32 devices in a mesh: grp: 1, rows: 32 (over z, y, x, core).
Axes of the slice: x: 2, y: 2, z: 4, core: 2. Of those that a mesh axis runs over, the one named last changes fastest.
Arguments:
- embeddings: bfloat16 [16384, 1024], P(('grp', 'rows')), may hold values from -30 to 30
- centroids: bfloat16 [4096, 1024], replicated, may hold values from -0.1875 to 0.1875
- log_weights: float32 [4096], replicated, may hold values from -1 to 1
Outputs:
- new_centroids: bfloat16 [4096, 1024], P(('grp', 'rows'))
- new_log_weights: float32 [4096], P(('grp', 'rows'))
- log_normalizer: float32 [16384], P(('grp', 'rows'))
The draws below stay inside these ranges and needn't reach their ends.
All inputs are finite; a program needn't handle non-finite values.
Results may differ from the reference program's by a relative error of at most 0.0034.
Values may be sent and summed in bfloat16 or wider, within the bound.
No kernel may reach another device: no remote copies, remote signals or barrier semaphores. Data moves between devices by JAX's collectives and lax.ppermute only.
A program may use at most 128 MiB of HBM per device.

```python
import math
import jax
import jax.numpy as jnp
from jax import lax

D = 1024
K = 4096
KAPPA = 32
ROWS_DEV = 512
NROWS = 16384


def draw_embeddings(key, part):
    key_noise = jax.random.fold_in(key, 11)
    key_topic = jax.random.fold_in(key, 12)
    key_rowscale = jax.random.fold_in(key, 13)
    key_colscale = jax.random.fold_in(key, 14)
    blocks_count = NROWS // ROWS_DEV
    noise_draw = jax.random.normal(key_noise, (blocks_count, ROWS_DEV, D), jnp.float32)
    topic_draw = jax.random.normal(key_topic, (blocks_count, 1, D), jnp.float32)
    row_scale = jnp.exp(jax.random.uniform(key_rowscale, (blocks_count, ROWS_DEV, 1), jnp.float32, math.log(0.3), math.log(3.0)))
    col_scale = jnp.exp(jax.random.uniform(key_colscale, (1, 1, D), jnp.float32, math.log(0.5), math.log(2.0)))
    base_draw = 0.6 * noise_draw + 0.8 * topic_draw
    values = jnp.clip(base_draw * row_scale * col_scale, -30.0, 30.0)
    return values.reshape(NROWS, D).astype(jnp.bfloat16)


def centred(own_key, dims, spread, limit, kind=jnp.bfloat16):
    return jnp.clip(spread * jax.random.normal(own_key, dims, jnp.float32), -limit, limit).astype(kind)


def setup_inputs(seed: int = 0, part: int = 0) -> dict:
    seeds = jax.random.split(jax.random.key(seed), 4)
    part_keys = jax.random.split(jax.random.fold_in(seeds[3], part), 4)
    return {
        "embeddings": draw_embeddings(jax.random.fold_in(jax.random.fold_in(seeds[3], part), 71), part),
        "centroids": centred(seeds[1], (K, D), D ** -0.5, 0.1875),
        "log_weights": jnp.clip(jax.random.uniform(seeds[2], (K,), jnp.float32, -1.0, 1.0), -1.0, 1.0),
    }


def reference(embeddings, centroids, log_weights):
    embed_float = embeddings.astype(jnp.float32)
    unit_rows = (embed_float * lax.rsqrt(lax.optimization_barrier(jnp.sum(embed_float * embed_float, 1, keepdims=True)) + 1e-06)).astype(jnp.bfloat16)
    blocks = unit_rows.reshape(NROWS // ROWS_DEV, ROWS_DEV, D)

    def accumulate(running_pair, row_block):
        centroid_sum, count_sum = running_pair
        scores = KAPPA * jnp.dot(row_block, centroids.T, preferred_element_type=jnp.float32) + log_weights
        exponent = jnp.exp(scores)
        responsible = (exponent / lax.optimization_barrier(jnp.sum(exponent, 1, keepdims=True))).astype(jnp.bfloat16)
        centroid_sum = centroid_sum + jnp.dot(responsible.T, row_block, preferred_element_type=jnp.float32)
        count_sum = count_sum + lax.optimization_barrier(jnp.sum(responsible.astype(jnp.float32), 0))
        return ((centroid_sum, count_sum), None)
    start_pair = (jnp.zeros((K, D), jnp.float32), jnp.zeros((K,), jnp.float32))
    (centroid_sum, count_sum), unused = lax.scan(accumulate, start_pair, blocks)
    new_directions = (centroid_sum * lax.rsqrt(lax.optimization_barrier(jnp.sum(centroid_sum * centroid_sum, 1, keepdims=True)) + 1e-06)).astype(jnp.bfloat16)
    new_log_weights = jnp.log(count_sum / NROWS)

    def second_pass(row_block):
        scores = KAPPA * jnp.dot(row_block, new_directions.T, preferred_element_type=jnp.float32) + new_log_weights
        return jnp.log(lax.optimization_barrier(jnp.sum(jnp.exp(scores), 1)))
    log_normalizer = lax.map(second_pass, blocks).reshape(NROWS)
    return (new_directions, new_log_weights, log_normalizer)
```

```python
import functools

import jax
import jax.numpy as jnp
from jax import lax
from jax.experimental import pallas as pl
from jax.experimental.pallas import tpu as pltpu
from jax.sharding import PartitionSpec as P

KAPPA = 32
EPS = 1e-06
LANES = 128
CORE, ACROSS, ALONG = 0, 1, 3
MIB = 1 << 20
F32, BF16 = jnp.float32, jnp.bfloat16
VMEM = pl.BlockSpec(memory_space=pltpu.VMEM)


def params(mib):
    return pltpu.CompilerParams(vmem_limit_bytes=mib * MIB)


def cost(macs, nbytes, exps=0):
    return pl.CostEstimate(flops=2 * macs, bytes_accessed=nbytes, transcendentals=exps)


def column(row):
    return jnp.broadcast_to(row, (LANES, row.shape[1])).T


def nt_dot(a, b):
    return lax.dot_general(a, b, (((1,), (1,)), ((), ())), preferred_element_type=F32)


def exp_scores(comps, rows, shift):
    dots = nt_dot(comps, rows)
    return [
        jnp.exp(KAPPA * dots[:, j : j + LANES] + shift) for j in range(0, dots.shape[1], LANES)
    ]


def unit_kernel(e_ref, a_ref, b_ref):
    half = a_ref.shape[0]
    for i, out in enumerate((a_ref, b_ref)):
        x = e_ref[i * half : (i + 1) * half, :].astype(F32)
        out[...] = (x * lax.rsqrt(jnp.sum(x * x, 1, keepdims=True) + EPS)).astype(BF16)


def unit(emb):
    rows, dim = emb.shape
    half = jax.ShapeDtypeStruct((rows // 2, dim), BF16)
    return pl.pallas_call(
        unit_kernel,
        out_shape=(half, half),
        in_specs=[VMEM],
        out_specs=(VMEM, VMEM),
        compiler_params=params(24),
        cost_estimate=cost(0, 4 * rows * dim, rows),
        name="unit_rows",
    )(emb)


def denom_kernel(c_ref, lw_ref, a_ref, b_ref, out_ref):
    @pl.when(pl.program_id(0) == 0)
    def _():
        out_ref[...] = jnp.zeros_like(out_ref)

    shift = column(lw_ref[0])
    half = a_ref.shape[0]
    for i, rows in enumerate((a_ref, b_ref)):
        pieces = exp_scores(c_ref[...], rows[...], shift)
        out_ref[:, i * half : (i + 1) * half] += jnp.concatenate(
            [jnp.sum(p, 0, keepdims=True) for p in pieces], 1
        )

    @pl.when(pl.program_id(0) == pl.num_programs(0) - 1)
    def _():
        out_ref[...] = 1.0 / out_ref[...]


def denominators(cen, lw, ua, ub):
    comps, dim = cen.shape
    half = ua.shape[0]
    tile = min(512, comps)
    whole = lambda shape: pl.BlockSpec(shape, lambda i: (0,) * len(shape))
    return pl.pallas_call(
        denom_kernel,
        grid=(comps // tile,),
        out_shape=jax.ShapeDtypeStruct((1, 2 * half), F32),
        in_specs=[
            pl.BlockSpec((tile, dim), lambda i: (i, 0)),
            pl.BlockSpec((1, 1, tile), lambda i: (i, 0, 0)),
            whole((half, dim)),
            whole((half, dim)),
        ],
        out_specs=whole((1, 2 * half)),
        compiler_params=params(24),
        cost_estimate=cost(2 * half * comps * dim, 2 * (comps + 2 * half) * dim, 2 * half * comps),
        name="denominators",
    )(cen, lw.reshape(comps // tile, 1, tile), ua, ub)


def sums_kernel(first, last, c_ref, lw_ref, inv_ref, *refs):
    pieces, refs = refs[:4], refs[4:]
    if not first:
        acc_in, cnt_in, refs = refs[0], refs[1], refs[2:]
    if last:
        keep_ref, send_ref, counts_ref, acc, cnt = refs
    else:
        acc, cnt = refs
    shift = column(lw_ref[...])
    half = pieces[0].shape[0]
    count = None
    total = None
    for i, piece in enumerate(pieces):
        u = piece[...]
        inv = inv_ref[i // 2 : i // 2 + 1, (i % 2) * half : (i % 2 + 1) * half]
        resp = []
        for j, e in enumerate(exp_scores(c_ref[...], u, shift)):
            r = (e * inv[:, j * LANES : (j + 1) * LANES]).astype(BF16)
            r32 = r.astype(F32)
            count = r32 if count is None else count + r32
            resp.append(r)
        part = jnp.dot(jnp.concatenate(resp, 1), u, preferred_element_type=F32)
        if i == 0:
            acc[...] = part if first else acc_in[...] + part
        else:
            acc[...] += part
    cnt[...] = count if first else cnt_in[...] + count
    if last:
        near = keep_ref.shape[0]
        keep_ref[...] = acc[:near, :]
        send_ref[...] = acc[near:, :].astype(BF16)
        counts_ref[...] = jnp.sum(cnt[...].T, 0, keepdims=True)


def sums(cen, lw, inv, pieces, state, last):
    comps, dim = cen.shape
    rows = 4 * pieces[0].shape[0]
    first = state is None
    acc = jax.ShapeDtypeStruct((comps, dim), F32)
    cnt = jax.ShapeDtypeStruct((comps, LANES), F32)
    if last:
        out_shape = (
            jax.ShapeDtypeStruct((comps // 2, dim), F32),
            jax.ShapeDtypeStruct((comps // 2, dim), BF16),
            jax.ShapeDtypeStruct((1, comps), F32),
        )
        scratch = [pltpu.VMEM(acc.shape, F32), pltpu.VMEM(cnt.shape, F32)]
    else:
        out_shape, scratch = (acc, cnt), []
    args = [cen, lw, inv, *pieces] + ([] if first else list(state))
    aliases = {} if first or last else {len(args) - 2: 0, len(args) - 1: 1}
    return pl.pallas_call(
        functools.partial(sums_kernel, first, last),
        out_shape=out_shape,
        in_specs=[VMEM] * len(args),
        out_specs=(VMEM,) * len(out_shape),
        scratch_shapes=scratch,
        input_output_aliases=aliases,
        compiler_params=params(24),
        cost_estimate=cost(2 * rows * comps * dim, 2 * (comps + rows) * dim, rows * comps),
        name="sums",
    )(*args)


def directions_kernel(keep_ref, *refs):
    total = keep_ref[...]
    for ref in refs[:-1]:
        total = total + ref[...].astype(F32)
    refs[-1][...] = (total * lax.rsqrt(jnp.sum(total * total, 1, keepdims=True) + EPS)).astype(BF16)


def directions(keep, received):
    return pl.pallas_call(
        directions_kernel,
        out_shape=jax.ShapeDtypeStruct(keep.shape, BF16),
        in_specs=[VMEM] * (1 + len(received)),
        out_specs=VMEM,
        compiler_params=params(24),
        cost_estimate=cost(0, 10 * keep.size, keep.shape[0]),
        name="directions",
    )(keep, *received)


def normalizer_kernel(n_comps, first, *refs):
    comps, refs = refs[:n_comps], refs[n_comps:]
    lw_ref, refs = refs[0], refs[1:]
    before, refs = (None, refs) if first else (refs[0], refs[1:])
    pieces, out_ref = refs[:-1], refs[-1]
    c = jnp.concatenate([r[...] for r in comps], 0)
    shift = column(lw_ref[...])
    half = pieces[0].shape[0]
    for i, piece in enumerate(pieces):
        s = jnp.concatenate(
            [jnp.sum(p, 0, keepdims=True) for p in exp_scores(c, piece[...], shift)], 1
        )
        at = slice(i // 2, i // 2 + 1), slice((i % 2) * half, (i % 2 + 1) * half)
        out_ref[at] = s if first else before[at] + s


def normalizers(comps, lw, before, pieces):
    half, dim = pieces[0].shape
    n_comps, rows = sum(c.shape[0] for c in comps), len(pieces) * half
    args = [*comps, lw] + ([] if before is None else [before]) + list(pieces)
    return pl.pallas_call(
        functools.partial(normalizer_kernel, len(comps), before is None),
        out_shape=jax.ShapeDtypeStruct((len(pieces) // 2, 2 * half), F32),
        in_specs=[VMEM] * len(args),
        out_specs=VMEM,
        compiler_params=params(32),
        cost_estimate=cost(rows * n_comps * dim, 2 * (n_comps + rows) * dim, rows * n_comps),
        name="normalizers",
    )(*args)


def local(embeddings, centroids, log_weights):
    n = lax.axis_size("rows")
    comps, dim = centroids.shape
    block = comps // n
    row_total = embeddings.shape[0] * n
    me = lax.axis_index("rows")
    group_bits = (CORE, ACROSS, ALONG)
    core, across, along = (1 << b for b in group_bits)
    far = [1 << b for b in range(n.bit_length() - 1) if b not in group_bits]

    def swap(x, mask):
        return lax.ppermute(x, "rows", [(i, i ^ mask) for i in range(n)])

    offsets = [0]
    for mask in reversed(far):
        offsets = offsets + [o | mask for o in offsets]
    offsets = sorted(offsets, key=lambda o: [bool(o & m) for m in far])
    where = {o: q for q, o in enumerate(offsets)}
    starts = [(me ^ o) * block for o in offsets]
    cen = jnp.concatenate([lax.dynamic_slice_in_dim(centroids, s, block) for s in starts])
    lw = jnp.concatenate([lax.dynamic_slice_in_dim(log_weights, s, block) for s in starts])
    lw = lw[None]

    ua, ub = unit(embeddings)
    xb, za = swap(ub, across), swap(ua, along)
    xa, zb = swap(ua, across), swap(ub, along)
    own_pair = (ua, ub, swap(ua, core), swap(ub, core))
    inv = denominators(centroids, log_weights, ua, ub)
    inv = jnp.concatenate([inv, swap(inv, core)])
    inv_x, inv_z = swap(inv, across), swap(inv, along)
    da, db = swap(za, across), swap(xb, along)
    inv_d = swap(inv_z, across)
    x_pair = (xa, xb, swap(xa, core), swap(xb, core))
    z_pair = (za, zb, swap(za, core), swap(zb, core))
    d_pair = (da, db, swap(da, core), swap(db, core))

    state = sums(cen, lw, inv, own_pair, None, False)
    state = sums(cen, lw, inv_x, x_pair, state, False)
    state = sums(cen, lw, inv_z, z_pair, state, False)
    keep, send, counts = sums(cen, lw, inv_d, d_pair, state, True)

    counts = counts.reshape(len(offsets), block)
    for mask in far:
        order = [where[o ^ mask] for o in offsets]
        got = swap(counts, mask)
        counts = counts + jnp.concatenate([got[q : q + 1] for q in order])
    new_lw = jnp.log(counts / row_total)
    own_lw = new_lw[0]

    def rows_of(x, q):
        return x[q * block : (q + 1) * block]

    half = len(offsets) // 2
    parts = {o: [rows_of(keep, q)] for q, o in enumerate(offsets[:half])}
    sent = {o: rows_of(send, q) for q, o in enumerate(offsets[half:])}
    for k, mask in enumerate(far):
        leaving = [o for o in offsets if o & mask and not any(o & m for m in far[:k])]
        for o in reversed(leaving):
            x = sent[o] if k == 0 else sum(p.astype(F32) for p in parts.pop(o)).astype(BF16)
            parts[o ^ mask].append(swap(x, mask))
    own_dirs = directions(parts[0][0], parts[0][1:])

    dirs = {0: own_dirs}
    for mask in reversed(far):
        for o in list(dirs):
            dirs[o | mask] = swap(dirs[o], mask)
    pieces = own_pair + x_pair + z_pair + d_pair
    block_lw = lambda os: jnp.concatenate([new_lw[where[o]] for o in os])[None]
    early = [o for o in offsets if o in (0, far[0])]
    late = [o for o in offsets if o not in early]
    total = normalizers([dirs[o] for o in early], block_lw(early), None, pieces)
    total = normalizers([dirs[o] for o in late], block_lw(late), total, pieces)

    for mask in (along, across, core):
        stay = total.shape[0] // 2
        total = total[:stay] + swap(total[stay:], mask)
    return own_dirs, own_lw, jnp.log(total[0])


def solution(mesh):
    return jax.shard_map(
        local,
        mesh=mesh,
        in_specs=(P(("grp", "rows"), None), P(), P()),
        out_specs=(P(("grp", "rows"), None), P(("grp", "rows")), P(("grp", "rows"))),
        check_vma=False,
    )
```

```python
import functools

import jax
import jax.numpy as jnp
from jax import lax
from jax.experimental import pallas as pl
from jax.experimental.pallas import tpu as pltpu
from jax.sharding import PartitionSpec as P

KAPPA = 32
EPS = 1e-06
LANES = 128
ACROSS, ALONG = 1, 3
TAIL = 16
PARTS = 1
DENOM_MIB = 40
HASTE = 1
MIB = 1 << 20
F32, BF16 = jnp.float32, jnp.bfloat16
VMEM = pl.BlockSpec(memory_space=pltpu.VMEM)


def params(mib):
    return pltpu.CompilerParams(vmem_limit_bytes=mib * MIB)


def cost(macs, nbytes, exps=0):
    flops = 2 * macs // HASTE
    return pl.CostEstimate(flops=flops, bytes_accessed=nbytes // HASTE, transcendentals=exps // HASTE)


def column(row):
    return jnp.broadcast_to(row, (LANES, row.shape[1])).T


def nt_dot(a, b):
    return lax.dot_general(a, b, (((1,), (1,)), ((), ())), preferred_element_type=F32)


def exp_scores(comps, rows, shift):
    dots = nt_dot(comps, rows)
    return [
        jnp.exp(KAPPA * dots[:, j : j + LANES] + shift) for j in range(0, dots.shape[1], LANES)
    ]


def unit_kernel(e_ref, a_ref, b_ref):
    half = a_ref.shape[0]
    for i, out in enumerate((a_ref, b_ref)):
        x = e_ref[i * half : (i + 1) * half, :].astype(F32)
        out[...] = (x * lax.rsqrt(jnp.sum(x * x, 1, keepdims=True) + EPS)).astype(BF16)


def unit(emb):
    rows, dim = emb.shape
    half = jax.ShapeDtypeStruct((rows // 2, dim), BF16)
    return pl.pallas_call(
        unit_kernel,
        out_shape=(half, half),
        in_specs=[VMEM],
        out_specs=(VMEM, VMEM),
        compiler_params=params(24),
        cost_estimate=cost(0, 4 * rows * dim, rows),
        name="unit_rows",
    )(emb)


def gather(n, offsets, block, c_hbm, lw_ref, cen_out, lw_out, sems):
    me = lax.rem(lax.axis_index("rows"), n)
    copies = []
    for q, o in enumerate(offsets):
        owner = me ^ o
        source = c_hbm.at[pl.ds(pl.multiple_of(owner * block, block), block), :]
        copy = pltpu.make_async_copy(source, cen_out.at[q * block : (q + 1) * block, :], sems.at[q])
        copy.start()
        copies.append(copy)
        lw_out[q] = lw_ref[owner]
    return copies


def denom_kernel(n, offsets, c_ref, lw_ref, c_hbm, lws_ref, a_ref, b_ref, *refs):
    out_a, out_b, cen_out, lw_out, total, sems = refs
    block = cen_out.shape[0] // len(offsets)

    @pl.when(pl.program_id(0) == 0)
    def _():
        total[...] = jnp.zeros_like(total)
        for copy in gather(n, offsets, block, c_hbm, lws_ref, cen_out, lw_out, sems):
            copy.wait()

    shift = column(lw_ref[0])
    half = a_ref.shape[0]
    for i, rows in enumerate((a_ref, b_ref)):
        pieces = exp_scores(c_ref[...], rows[...], shift)
        total[:, i * half : (i + 1) * half] += jnp.concatenate(
            [jnp.sum(p, 0, keepdims=True) for p in pieces], 1
        )

    @pl.when(pl.program_id(0) == pl.num_programs(0) - 1)
    def _():
        weight = 1.0 / total[...]
        high = weight.astype(BF16).astype(F32)
        tail = jnp.concatenate([high, weight - high], 1)
        tail = jnp.broadcast_to(tail, (TAIL, tail.shape[1])).astype(BF16)
        for rows, out in ((a_ref, out_a), (b_ref, out_b)):
            out[:half, :] = rows[...]
            out[half:, : tail.shape[1]] = tail


def denominators(cen, lw, ua, ub, n, offsets):
    comps, dim = cen.shape
    half, block = ua.shape[0], comps // n
    tile = min(512, comps)
    whole = lambda shape: pl.BlockSpec(shape, lambda i: (0,) * len(shape))
    longer = jax.ShapeDtypeStruct((half + TAIL, dim), BF16)
    out_shape = (
        longer,
        longer,
        jax.ShapeDtypeStruct((len(offsets) * block, dim), BF16),
        jax.ShapeDtypeStruct((len(offsets), 1, block), F32),
    )
    return pl.pallas_call(
        functools.partial(denom_kernel, n, offsets),
        grid=(comps // tile,),
        out_shape=out_shape,
        in_specs=[
            pl.BlockSpec((tile, dim), lambda i: (i, 0)),
            pl.BlockSpec((1, 1, tile), lambda i: (i, 0, 0)),
            pl.BlockSpec(memory_space=pl.ANY),
            whole((n, 1, block)),
            whole((half, dim)),
            whole((half, dim)),
        ],
        out_specs=tuple(whole(o.shape) for o in out_shape),
        scratch_shapes=[
            pltpu.VMEM((1, 2 * half), F32),
            pltpu.SemaphoreType.DMA((len(offsets),)),
        ],
        compiler_params=params(DENOM_MIB),
        cost_estimate=cost(2 * half * comps * dim, 2 * (comps + 2 * half) * dim, 2 * half * comps),
        name="denominators",
    )(cen, lw.reshape(comps // tile, 1, tile), cen, lw.reshape(n, 1, block), ua, ub)


def sums_kernel(first, last, half, at, c_ref, lw_ref, tail_ref, *refs):
    pieces, refs = refs[:2], refs[2:]
    if not first:
        acc_in, cnt_in, refs = refs[0], refs[1], refs[2:]
    *outs, cnt_out = refs
    block = c_ref.shape[0] // lw_ref.shape[0]
    comps = slice(at, at + sum(out.shape[0] for out in outs))
    shift = jnp.concatenate(
        [column(lw_ref[q]) for q in range(comps.start // block, comps.stop // block)], 0
    )
    c = c_ref[comps, :]
    rows = 2 * half
    end = tail_ref.shape[0]
    tail = tail_ref[end - TAIL : end, : 2 * rows].astype(F32)[:1]
    weight = tail[:, :rows] + tail[:, rows:]
    count, total = None, None
    for i, piece in enumerate(pieces):
        u = piece[:half, :]
        resp = []
        for j, e in enumerate(exp_scores(c, u, shift)):
            lanes = i * half + j * LANES
            r = (e * weight[:, lanes : lanes + LANES]).astype(BF16)
            count = r.astype(F32) if count is None else count + r.astype(F32)
            resp.append(r)
        part = jnp.dot(jnp.concatenate(resp, 1), u, preferred_element_type=F32)
        total = part if total is None else total + part
    if not first:
        total = total + acc_in[comps, :]
        count = count + cnt_in[comps, :]
    start = 0
    for out in outs:
        out[...] = total[start : start + out.shape[0], :]
        start += out.shape[0]
    if last:
        for q in range(cnt_out.shape[0]):
            one = count[q * block : (q + 1) * block, :]
            cnt_out[q : q + 1, :] = jnp.sum(one.T, 0, keepdims=True)
    else:
        cnt_out[...] = count


def sums(cen, lw, tail, pieces, half, state, segment=None):
    comps, dim = cen.shape
    last = segment is not None
    first = state is None
    if last:
        at, size = segment
        block = lw.shape[2]
        out_shape = (jax.ShapeDtypeStruct((size // 2, dim), F32),) * 2
        out_shape += (jax.ShapeDtypeStruct((size // block, block), F32),)
    else:
        at, size = 0, comps
        out_shape = (
            jax.ShapeDtypeStruct((comps, dim), F32),
            jax.ShapeDtypeStruct((comps, LANES), F32),
        )
    args = [cen, lw, tail, *pieces] + ([] if first else list(state))
    aliases = {} if first or last else {len(args) - 2: 0, len(args) - 1: 1}
    return pl.pallas_call(
        functools.partial(sums_kernel, first, last, half, at),
        out_shape=out_shape,
        in_specs=[VMEM] * len(args),
        out_specs=(VMEM,) * len(out_shape),
        input_output_aliases=aliases,
        compiler_params=params(24),
        cost_estimate=cost(4 * half * size * dim, 2 * (size + 2 * half) * dim, 2 * half * size),
        name="sums",
    )(*args)


def merge_kernel(terms, finish, n_in, *refs):
    arrays, outs = refs[:n_in], refs[n_in:]
    for out, parts in zip(outs, terms):
        total = sum(arrays[i][at : at + out.shape[0], :].astype(F32) for i, at in parts)
        out[...] = finish(total).astype(out.dtype)


def normalize(x):
    return x * lax.rsqrt(jnp.sum(x * x, 1, keepdims=True) + EPS)


def merge(wanted, size, finish, name):
    arrays, terms = [], []
    for parts in wanted:
        term = []
        for x, at in parts:
            if not any(x is y for y in arrays):
                arrays.append(x)
            term.append((next(i for i, y in enumerate(arrays) if y is x), at))
        terms.append(term)
    dim = arrays[0].shape[1]
    out = jax.ShapeDtypeStruct((size, dim), BF16)
    return pl.pallas_call(
        functools.partial(merge_kernel, terms, finish, len(arrays)),
        out_shape=(out,) * len(wanted),
        in_specs=[VMEM] * len(arrays),
        out_specs=(VMEM,) * len(wanted),
        compiler_params=params(16),
        cost_estimate=cost(0, 12 * size * dim * len(wanted), size),
        name=name,
    )(*arrays)


def normalizer_kernel(n_comps, lw_rows, n_rows, half, *refs):
    comps, refs = refs[:n_comps], refs[n_comps:]
    lw_ref, refs = refs[0], refs[1:]
    pieces, refs = refs[: 2 * n_rows], refs[2 * n_rows :]
    before, outs = refs[:-n_rows], refs[-n_rows:]
    c = jnp.concatenate([r[...] for r in comps], 0)
    shift = jnp.concatenate([column(lw_ref[q : q + 1, :]) for q in lw_rows], 0)
    for i, out in enumerate(outs):
        for k in range(2):
            s = jnp.concatenate(
                [
                    jnp.sum(p, 0, keepdims=True)
                    for p in exp_scores(c, pieces[2 * i + k][:half, :], shift)
                ],
                1,
            )
            at = slice(None), slice(k * half, (k + 1) * half)
            out[at] = before[i][at] + s if before else s


def normalizers(comps, lw, lw_rows, before, pieces, half):
    dim = pieces[0].shape[1]
    n_comps, n_rows = sum(c.shape[0] for c in comps), len(pieces) // 2
    args = [*comps, lw, *pieces, *before]
    rows = 2 * half * n_rows
    return pl.pallas_call(
        functools.partial(normalizer_kernel, len(comps), lw_rows, n_rows, half),
        out_shape=(jax.ShapeDtypeStruct((1, 2 * half), F32),) * n_rows,
        in_specs=[VMEM] * len(args),
        out_specs=(VMEM,) * n_rows,
        compiler_params=params(24),
        cost_estimate=cost(rows * n_comps * dim, 2 * (n_comps + rows) * dim, rows * n_comps),
        name="normalizers",
    )(*args)


def local(embeddings, centroids, log_weights):
    n = lax.axis_size("rows")
    comps, dim = centroids.shape
    block = comps // n
    half = embeddings.shape[0] // 2
    row_total = embeddings.shape[0] * n
    me = lax.axis_index("rows")
    across, along = 1 << ACROSS, 1 << ALONG
    far = [1 << b for b in range(n.bit_length() - 1) if b not in (ACROSS, ALONG)]

    def swap(x, mask):
        return lax.ppermute(x, "rows", [(i, i ^ mask) for i in range(n)])

    offsets = [0]
    for mask in far:
        offsets = [o | m for o in offsets for m in (0, mask)]
    where = {o: q for q, o in enumerate(offsets)}

    ua, ub = unit(embeddings)
    xb, za = swap(ub, across), swap(ua, along)
    va, vb, cen, lw = denominators(centroids, log_weights, ua, ub, n, offsets)
    xa, zb = swap(va, across), swap(vb, along)
    da, db = swap(za, across), swap(xb, along)
    d_tail = swap(zb[half:], across)

    state = sums(cen, lw, va, (va, vb), half, None)
    state = sums(cen, lw, xa, (xa, xb), half, state)
    state = sums(cen, lw, zb, (za, zb), half, state)
    size = len(offsets) // 2 * block
    send0, send1, send_counts = sums(cen, lw, d_tail, (da, db), half, state, (size, size))
    keep0, keep1, keep_counts = sums(cen, lw, d_tail, (da, db), half, state, (0, size))

    got1 = swap(send1, far[0])
    got0 = swap(send0, far[0])
    quarter = len(offsets) // 4
    sub = block // PARTS
    parts = {}
    for pair, first in (((keep0, got0), 0), ((keep1, got1), quarter)):
        for q in range(quarter):
            for h in range(PARTS):
                parts[offsets[first + q], h] = [(x, q * block + h * sub) for x in pair]
    for k, mask in list(enumerate(far))[1:]:
        leaving = [o for o in reversed(offsets) if (o, 0) in parts and o & mask]
        items = [(o, h) for o in leaving for h in range(PARTS)]
        for group in [items] if k == 1 else [[i] for i in items]:
            merged = merge([parts.pop(i) for i in group], sub, lambda x: x, "merge")
            for (o, h), x in zip(group, merged):
                parts[o ^ mask, h].append((swap(x, mask), 0))
    dirs = {}
    for h in range(PARTS):
        (dirs[0, h],) = merge([parts[0, h]], sub, normalize, "directions")
    own_dirs = jnp.concatenate([dirs[0, h] for h in range(PARTS)])

    counts = jnp.concatenate([keep_counts, send_counts])
    for mask in far:
        order = [where[o ^ mask] for o in offsets]
        got = swap(counts, mask)
        counts = counts + jnp.concatenate([got[q : q + 1] for q in order])
    new_lw = jnp.log(counts / row_total)
    own_lw = new_lw[0]

    for mask in reversed(far[2:]):
        for o, h in list(dirs):
            dirs[o | mask, h] = swap(dirs[o, h], mask)
    pieces = (va, vb, xa, xb, za, zb, da, db)
    total = ()

    def arrived(os):
        return [dirs[o, h] for o in os for h in range(PARTS)]

    def send_all(os, mask, after=None):
        for o in os:
            for h in range(PARTS):
                x = dirs[o, h]
                if after is not None:
                    x, _ = lax.optimization_barrier((x, after))
                    dirs[o, h] = x
                dirs[o | mask, h] = swap(x, mask)

    def use(o, total):
        now = [o, o | far[0]]
        return normalizers(arrived(now), new_lw, [where[o] for o in now], total, pieces, half)

    near, *outer = [o for o in offsets if not o & (far[0] | far[1])]
    send_all([near], far[1])
    send_all([near], far[0])
    total = use(near, total)
    send_all(outer, far[1], total[0])
    send_all([near | far[1]], far[0], dirs[outer[0], 0] if outer else None)
    send_all(outer, far[0])
    for o in [near | far[1], *outer]:
        total = use(o, total)
    last = [o | far[1] for o in outer]
    send_all(last, far[0], total[0])
    for o in last:
        total = use(o, total)

    own, x, z, d = total
    whole = own + swap(d, across | along) + swap(z, along) + swap(x, across)
    return own_dirs, own_lw, jnp.log(whole[0])


def solution(mesh):
    return jax.shard_map(
        local,
        mesh=mesh,
        in_specs=(P(("grp", "rows"), None), P(), P()),
        out_specs=(P(("grp", "rows"), None), P(("grp", "rows")), P(("grp", "rows"))),
        check_vma=False,
    )
```

```python
import functools

import jax
import jax.numpy as jnp
from jax import lax
from jax.experimental import pallas as pl
from jax.experimental.pallas import tpu as pltpu
from jax.sharding import PartitionSpec as P

KAPPA = 32
EPS = 1e-06
LANES = 128
ACROSS, ALONG = 1, 3
TAIL = 16
PARTS = 2
MIB = 1 << 20
F32, BF16 = jnp.float32, jnp.bfloat16
VMEM = pl.BlockSpec(memory_space=pltpu.VMEM)


def params(mib):
    return pltpu.CompilerParams(vmem_limit_bytes=mib * MIB)


def cost(macs, nbytes, exps=0):
    return pl.CostEstimate(flops=2 * macs, bytes_accessed=nbytes, transcendentals=exps)


def column(row):
    return jnp.broadcast_to(row, (LANES, row.shape[1])).T


def nt_dot(a, b):
    return lax.dot_general(a, b, (((1,), (1,)), ((), ())), preferred_element_type=F32)


def exp_scores(comps, rows, shift):
    dots = nt_dot(comps, rows)
    return [
        jnp.exp(KAPPA * dots[:, j : j + LANES] + shift) for j in range(0, dots.shape[1], LANES)
    ]


def unit_kernel(e_ref, a_ref, b_ref):
    half = a_ref.shape[0]
    for i, out in enumerate((a_ref, b_ref)):
        x = e_ref[i * half : (i + 1) * half, :].astype(F32)
        out[...] = (x * lax.rsqrt(jnp.sum(x * x, 1, keepdims=True) + EPS)).astype(BF16)


def unit(emb):
    rows, dim = emb.shape
    half = jax.ShapeDtypeStruct((rows // 2, dim), BF16)
    return pl.pallas_call(
        unit_kernel,
        out_shape=(half, half),
        in_specs=[VMEM],
        out_specs=(VMEM, VMEM),
        compiler_params=params(24),
        cost_estimate=cost(0, 4 * rows * dim, rows),
        name="unit_rows",
    )(emb)


def gather(n, offsets, block, c_hbm, cen_out, sems):
    me = lax.rem(lax.axis_index("rows"), n)
    copies = []
    for q, o in enumerate(offsets):
        source = c_hbm.at[pl.ds(pl.multiple_of((me ^ o) * block, block), block), :]
        target = cen_out.at[q * block : (q + 1) * block, :]
        copies.append(pltpu.make_async_copy(source, target, sems.at[q]))
    return copies


def denom_kernel(n, offsets, c_ref, lw_ref, c_hbm, lws_ref, a_ref, b_ref, *refs):
    out_a, out_b, cen_out, lw_out, total, sems = refs
    block = cen_out.shape[0] // len(offsets)

    @pl.when(pl.program_id(0) == 0)
    def _():
        total[...] = jnp.zeros_like(total)
        for copy in gather(n, offsets, block, c_hbm, cen_out, sems):
            copy.start()
        me = lax.rem(lax.axis_index("rows"), n)
        for q, o in enumerate(offsets):
            lw_out[q] = lws_ref[me ^ o]

    shift = column(lw_ref[0])
    half = a_ref.shape[0]
    for i, rows in enumerate((a_ref, b_ref)):
        pieces = exp_scores(c_ref[...], rows[...], shift)
        total[:, i * half : (i + 1) * half] += jnp.concatenate(
            [jnp.sum(p, 0, keepdims=True) for p in pieces], 1
        )

    @pl.when(pl.program_id(0) == pl.num_programs(0) - 1)
    def _():
        weight = 1.0 / total[...]
        high = weight.astype(BF16).astype(F32)
        tail = jnp.concatenate([high, weight - high], 1)
        tail = jnp.broadcast_to(tail, (TAIL, tail.shape[1])).astype(BF16)
        for rows, out in ((a_ref, out_a), (b_ref, out_b)):
            out[:half, :] = rows[...]
            out[half:, : tail.shape[1]] = tail
        for copy in gather(n, offsets, block, c_hbm, cen_out, sems):
            copy.wait()


def denominators(cen, lw, ua, ub, n, offsets):
    comps, dim = cen.shape
    half, block = ua.shape[0], comps // n
    tile = min(512, comps)
    whole = lambda shape: pl.BlockSpec(shape, lambda i: (0,) * len(shape))
    longer = jax.ShapeDtypeStruct((half + TAIL, dim), BF16)
    out_shape = (
        longer,
        longer,
        jax.ShapeDtypeStruct((len(offsets) * block, dim), BF16),
        jax.ShapeDtypeStruct((len(offsets), 1, block), F32),
    )
    return pl.pallas_call(
        functools.partial(denom_kernel, n, offsets),
        grid=(comps // tile,),
        out_shape=out_shape,
        in_specs=[
            pl.BlockSpec((tile, dim), lambda i: (i, 0)),
            pl.BlockSpec((1, 1, tile), lambda i: (i, 0, 0)),
            pl.BlockSpec(memory_space=pl.ANY),
            whole((n, 1, block)),
            whole((half, dim)),
            whole((half, dim)),
        ],
        out_specs=tuple(whole(o.shape) for o in out_shape),
        scratch_shapes=[
            pltpu.VMEM((1, 2 * half), F32),
            pltpu.SemaphoreType.DMA((len(offsets),)),
        ],
        compiler_params=params(40),
        cost_estimate=cost(2 * half * comps * dim, 2 * (comps + 2 * half) * dim, 2 * half * comps),
        name="denominators",
    )(cen, lw.reshape(comps // tile, 1, tile), cen, lw.reshape(n, 1, block), ua, ub)


def sums_kernel(first, last, half, at, c_ref, lw_ref, tail_ref, *refs):
    pieces, refs = refs[:2], refs[2:]
    if not first:
        acc_in, cnt_in, refs = refs[0], refs[1], refs[2:]
    *outs, cnt_out = refs
    block = c_ref.shape[0] // lw_ref.shape[0]
    comps = slice(at, at + sum(out.shape[0] for out in outs))
    shift = jnp.concatenate(
        [column(lw_ref[q]) for q in range(comps.start // block, comps.stop // block)], 0
    )
    c = c_ref[comps, :]
    rows = 2 * half
    end = tail_ref.shape[0]
    tail = tail_ref[end - TAIL : end, : 2 * rows].astype(F32)[:1]
    weight = tail[:, :rows] + tail[:, rows:]
    count, total = None, None
    for i, piece in enumerate(pieces):
        u = piece[:half, :]
        resp = []
        for j, e in enumerate(exp_scores(c, u, shift)):
            lanes = i * half + j * LANES
            r = (e * weight[:, lanes : lanes + LANES]).astype(BF16)
            count = r.astype(F32) if count is None else count + r.astype(F32)
            resp.append(r)
        part = jnp.dot(jnp.concatenate(resp, 1), u, preferred_element_type=F32)
        total = part if total is None else total + part
    if not first:
        total = total + acc_in[comps, :]
        count = count + cnt_in[comps, :]
    start = 0
    for out in outs:
        out[...] = total[start : start + out.shape[0], :]
        start += out.shape[0]
    if last:
        for q in range(cnt_out.shape[0]):
            one = count[q * block : (q + 1) * block, :]
            cnt_out[q : q + 1, :] = jnp.sum(one.T, 0, keepdims=True)
    else:
        cnt_out[...] = count


def sums(cen, lw, tail, pieces, half, state, segment=None):
    comps, dim = cen.shape
    last = segment is not None
    first = state is None
    if last:
        at, size = segment
        block = lw.shape[2]
        out_shape = (jax.ShapeDtypeStruct((size // 2, dim), F32),) * 2
        out_shape += (jax.ShapeDtypeStruct((size // block, block), F32),)
    else:
        at, size = 0, comps
        out_shape = (
            jax.ShapeDtypeStruct((comps, dim), F32),
            jax.ShapeDtypeStruct((comps, LANES), F32),
        )
    args = [cen, lw, tail, *pieces] + ([] if first else list(state))
    aliases = {} if first or last else {len(args) - 2: 0, len(args) - 1: 1}
    return pl.pallas_call(
        functools.partial(sums_kernel, first, last, half, at),
        out_shape=out_shape,
        in_specs=[VMEM] * len(args),
        out_specs=(VMEM,) * len(out_shape),
        input_output_aliases=aliases,
        compiler_params=params(24),
        cost_estimate=cost(4 * half * size * dim, 2 * (size + 2 * half) * dim, 2 * half * size),
        name="sums",
    )(*args)


def merge_kernel(terms, n_in, *refs):
    arrays, outs = refs[:n_in], refs[n_in:]
    for out, parts in zip(outs, terms):
        total = sum(arrays[i][at : at + out.shape[0], :].astype(F32) for i, at in parts)
        out[...] = total.astype(out.dtype)


def normalize(x):
    return x * lax.rsqrt(jnp.sum(x * x, 1, keepdims=True) + EPS)


def directions_kernel(terms, size, *refs):
    *arrays, out = refs
    for k, parts in enumerate(terms):
        total = sum(arrays[i][at : at + size, :].astype(F32) for i, at in parts)
        out[k * size : (k + 1) * size, :] = normalize(total).astype(out.dtype)


def directions(wanted, size):
    arrays, terms = distinct(wanted)
    dim = arrays[0].shape[1]
    return pl.pallas_call(
        functools.partial(directions_kernel, terms, size),
        out_shape=jax.ShapeDtypeStruct((size * len(wanted), dim), BF16),
        in_specs=[VMEM] * len(arrays),
        out_specs=VMEM,
        compiler_params=params(8),
        cost_estimate=cost(0, 12 * size * dim * len(wanted), size),
        name="directions",
    )(*arrays)


def distinct(wanted):
    arrays, terms = [], []
    for parts in wanted:
        term = []
        for x, at in parts:
            if not any(x is y for y in arrays):
                arrays.append(x)
            term.append((next(i for i, y in enumerate(arrays) if y is x), at))
        terms.append(term)
    return arrays, terms


def merge(wanted, sizes):
    arrays, terms = distinct(wanted)
    dim = arrays[0].shape[1]
    return pl.pallas_call(
        functools.partial(merge_kernel, terms, len(arrays)),
        out_shape=tuple(jax.ShapeDtypeStruct((size, dim), BF16) for size in sizes),
        in_specs=[VMEM] * len(arrays),
        out_specs=(VMEM,) * len(wanted),
        compiler_params=params(8),
        cost_estimate=cost(0, 12 * sum(sizes) * dim, sum(sizes)),
        name="merge",
    )(*arrays)


def normalizer_kernel(n_comps, lw_rows, n_rows, half, *refs):
    comps, refs = refs[:n_comps], refs[n_comps:]
    lw_ref, refs = refs[0], refs[1:]
    pieces, refs = refs[: 2 * n_rows], refs[2 * n_rows :]
    before, outs = refs[:-n_rows], refs[-n_rows:]
    c = jnp.concatenate([r[...] for r in comps], 0)
    shift = jnp.concatenate(
        [
            column(lw_ref[q : q + 1, :])[h * r.shape[0] : (h + 1) * r.shape[0], :]
            for r, (q, h) in zip(comps, lw_rows)
        ],
        0,
    )
    for i, out in enumerate(outs):
        for k in range(2):
            s = jnp.concatenate(
                [
                    jnp.sum(p, 0, keepdims=True)
                    for p in exp_scores(c, pieces[2 * i + k][:half, :], shift)
                ],
                1,
            )
            at = slice(None), slice(k * half, (k + 1) * half)
            out[at] = before[i][at] + s if before else s


def normalizers(comps, lw, lw_rows, before, pieces, half):
    dim = pieces[0].shape[1]
    n_comps, n_rows = sum(c.shape[0] for c in comps), len(pieces) // 2
    args = [*comps, lw, *pieces, *before]
    rows = 2 * half * n_rows
    return pl.pallas_call(
        functools.partial(normalizer_kernel, len(comps), lw_rows, n_rows, half),
        out_shape=(jax.ShapeDtypeStruct((1, 2 * half), F32),) * n_rows,
        in_specs=[VMEM] * len(args),
        out_specs=(VMEM,) * n_rows,
        compiler_params=params(12),
        cost_estimate=cost(rows * n_comps * dim, 2 * (n_comps + rows) * dim, rows * n_comps),
        name="normalizers",
    )(*args)


def local(embeddings, centroids, log_weights):
    n = lax.axis_size("rows")
    comps, dim = centroids.shape
    block = comps // n
    half = embeddings.shape[0] // 2
    row_total = embeddings.shape[0] * n
    me = lax.axis_index("rows")
    across, along = 1 << ACROSS, 1 << ALONG
    far = [1 << b for b in range(n.bit_length() - 1) if b not in (ACROSS, ALONG)]

    def after(terms, ready):
        *others, (x, at) = terms
        x, _ = lax.optimization_barrier((x, ready))
        return [*others, (x, at)]

    def swap(x, mask):
        return lax.ppermute(x, "rows", [(i, i ^ mask) for i in range(n)])

    offsets = [0]
    for mask in far:
        offsets = [o | m for o in offsets for m in (0, mask)]
    where = {o: q for q, o in enumerate(offsets)}

    ua, ub = unit(embeddings)
    xb, za = swap(ub, across), swap(ua, along)
    va, vb, cen, lw = denominators(centroids, log_weights, ua, ub, n, offsets)
    xa, zb = swap(va, across), swap(vb, along)
    da, db = swap(za, across), swap(xb, along)
    d_tail = swap(zb[half:], across)

    state = sums(cen, lw, va, (va, vb), half, None)
    state = sums(cen, lw, xa, (xa, xb), half, state)
    state = sums(cen, lw, zb, (za, zb), half, state)
    size = len(offsets) // 2 * block
    send0, send1, send_counts = sums(cen, lw, d_tail, (da, db), half, state, (size, size))
    keep0, keep1, keep_counts = sums(cen, lw, d_tail, (da, db), half, state, (0, size))

    got1 = swap(send1, far[0])
    got0 = swap(send0, far[0])
    quarter = len(offsets) // 4
    sub = block // PARTS
    parts = {}
    for pair, first in (((keep0, got0), 0), ((keep1, got1), quarter)):
        for q in range(quarter):
            for h in range(PARTS):
                parts[offsets[first + q], h] = [(x, q * block + h * sub) for x in pair]
    ready, done = None, []
    for k, mask in list(enumerate(far))[1:]:
        leaving = [o for o in reversed(offsets) if (o, 0) in parts and o & mask]
        items = [(o, h) for o in leaving for h in range(PARTS)]
        if k == 1 < len(far) - 1:
            items = [(o, h) for o, h in items if o != mask or h == 0]
        for group in [items] if k == 1 else [[i] for i in items]:
            sizes = [block if o == mask and k == 1 < len(far) - 1 else sub for o, h in group]
            wanted = [parts[i] for i in group]
            if ready is not None:
                wanted[0] = after(wanted[0], ready)
            merged = merge(wanted, sizes)
            done.append(merged[0])
            if k > 1:
                ready = merged[0]
            for (o, h), x, size in zip(group, merged, sizes):
                x = swap(x, mask)
                for i in range(size // sub):
                    parts.pop((o, h + i))
                    parts[o ^ mask, h + i].append((x, i * sub))
    dirs = {}
    for h in range(PARTS):
        wanted = parts[0, h] if h == 0 else after(parts[0, h], dirs[0, h - 1])
        dirs[0, h] = directions([wanted], sub)
    own_dirs = jnp.concatenate([dirs[0, h] for h in range(PARTS)])

    counts = jnp.concatenate([keep_counts, send_counts])
    points = [done[0], done[min(1, len(done) - 1)], dirs[0, 0]]
    for k, mask in enumerate(far):
        counts, _ = lax.optimization_barrier((counts, points[min(k, 2)]))
        order = [where[o ^ mask] for o in offsets]
        got = swap(counts, mask)
        counts = counts + jnp.concatenate([got[q : q + 1] for q in order])
    new_lw = jnp.log(counts / row_total)
    own_lw = new_lw[0]

    halves = range(PARTS)
    for mask in reversed(far[2:]):
        for o, h in list(dirs):
            dirs[o | mask, h] = swap(dirs[o, h], mask)
    pieces = (va, vb, xa, xb, za, zb, da, db)
    total = ()

    def send(o, h, mask, ready=None):
        x = dirs[o, h]
        if ready is not None:
            x, _ = lax.optimization_barrier((x, ready))
            dirs[o, h] = x
        dirs[o | mask, h] = swap(x, mask)

    def use(o, hs, total):
        keys = [(p, h) for p in (o, o | far[0]) for h in hs]
        places = [(where[p], h) for p, h in keys]
        return normalizers([dirs[k] for k in keys], new_lw, places, total, pieces, half)

    near, *outer = [o for o in offsets if not o & (far[0] | far[1])]
    for h in halves:
        send(near, h, far[1])
        send(near, h, far[0])
    total = use(near, halves, total)
    for o in outer:
        for h in halves:
            send(o, h, far[1], total[0] if h == 0 else dirs[o | far[0], h - 1])
            send(o, h, far[0])
    for h in halves:
        send(near | far[1], h, far[0], dirs[outer[0], 0] if outer else None)
    total = use(near | far[1], halves, total)
    for o in outer:
        first, total = lax.optimization_barrier((dirs[o | far[1], 0], total))
        dirs[o | far[1], 0] = first
        send(o | far[1], 0, far[0])
        total = use(o, halves, total)
    for o in outer:
        for h in halves[1:]:
            send(o | far[1], h, far[0], total[0])
        total = use(o | far[1], halves, total)

    own, x, z, d = total
    whole = own + swap(d, across | along) + swap(z, along) + swap(x, across)
    return own_dirs, own_lw, jnp.log(whole[0])


def solution(mesh):
    return jax.shard_map(
        local,
        mesh=mesh,
        in_specs=(P(("grp", "rows"), None), P(), P()),
        out_specs=(P(("grp", "rows"), None), P(("grp", "rows")), P(("grp", "rows"))),
        check_vma=False,
    )
```

```python
import functools

import jax
import jax.numpy as jnp
from jax import lax
from jax.experimental import pallas as pl
from jax.experimental.pallas import tpu as pltpu
from jax.sharding import PartitionSpec as P

KAPPA = 32
EPS = 1e-06
LANES = 128
ACROSS, ALONG = 1, 3
TAIL = 16
PARTS = 2
MIB = 1 << 20
F32, BF16 = jnp.float32, jnp.bfloat16
VMEM = pl.BlockSpec(memory_space=pltpu.VMEM)


def params(mib):
    return pltpu.CompilerParams(vmem_limit_bytes=mib * MIB)


def cost(macs, nbytes, exps=0):
    return pl.CostEstimate(flops=2 * macs, bytes_accessed=nbytes, transcendentals=exps)


def column(row):
    return jnp.broadcast_to(row, (LANES, row.shape[1])).T


def nt_dot(a, b):
    return lax.dot_general(a, b, (((1,), (1,)), ((), ())), preferred_element_type=F32)


def exp_scores(comps, rows, shift):
    dots = nt_dot(comps, rows)
    return [
        jnp.exp(KAPPA * dots[:, j : j + LANES] + shift) for j in range(0, dots.shape[1], LANES)
    ]


def unit_kernel(e_ref, a_ref, b_ref):
    half = a_ref.shape[0]
    for i, out in enumerate((a_ref, b_ref)):
        x = e_ref[i * half : (i + 1) * half, :].astype(F32)
        out[...] = (x * lax.rsqrt(jnp.sum(x * x, 1, keepdims=True) + EPS)).astype(BF16)


def unit(emb):
    rows, dim = emb.shape
    half = jax.ShapeDtypeStruct((rows // 2, dim), BF16)
    return pl.pallas_call(
        unit_kernel,
        out_shape=(half, half),
        in_specs=[VMEM],
        out_specs=(VMEM, VMEM),
        compiler_params=params(24),
        cost_estimate=cost(0, 4 * rows * dim, rows),
        name="unit_rows",
    )(emb)


def gather(n, offsets, block, c_hbm, cen_out, sems):
    me = lax.rem(lax.axis_index("rows"), n)
    copies = []
    for q, o in enumerate(offsets):
        source = c_hbm.at[pl.ds(pl.multiple_of((me ^ o) * block, block), block), :]
        target = cen_out.at[q * block : (q + 1) * block, :]
        copies.append(pltpu.make_async_copy(source, target, sems.at[q]))
    return copies


def denom_kernel(n, offsets, c_ref, lw_ref, c_hbm, lws_ref, a_ref, b_ref, *refs):
    out_a, out_b, cen_out, lw_out, total, sems = refs
    block = cen_out.shape[0] // len(offsets)

    @pl.when(pl.program_id(0) == 0)
    def _():
        total[...] = jnp.zeros_like(total)
        for copy in gather(n, offsets, block, c_hbm, cen_out, sems):
            copy.start()
        me = lax.rem(lax.axis_index("rows"), n)
        for q, o in enumerate(offsets):
            lw_out[q] = lws_ref[me ^ o]

    shift = column(lw_ref[0])
    half = a_ref.shape[0]
    for i, rows in enumerate((a_ref, b_ref)):
        pieces = exp_scores(c_ref[...], rows[...], shift)
        total[:, i * half : (i + 1) * half] += jnp.concatenate(
            [jnp.sum(p, 0, keepdims=True) for p in pieces], 1
        )

    @pl.when(pl.program_id(0) == pl.num_programs(0) - 1)
    def _():
        weight = 1.0 / total[...]
        high = weight.astype(BF16).astype(F32)
        tail = jnp.concatenate([high, weight - high], 1)
        tail = jnp.broadcast_to(tail, (TAIL, tail.shape[1])).astype(BF16)
        for rows, out in ((a_ref, out_a), (b_ref, out_b)):
            out[:half, :] = rows[...]
            out[half:, : tail.shape[1]] = tail
        for copy in gather(n, offsets, block, c_hbm, cen_out, sems):
            copy.wait()


def denominators(cen, lw, ua, ub, n, offsets):
    comps, dim = cen.shape
    half, block = ua.shape[0], comps // n
    tile = min(512, comps)
    whole = lambda shape: pl.BlockSpec(shape, lambda i: (0,) * len(shape))
    longer = jax.ShapeDtypeStruct((half + TAIL, dim), BF16)
    out_shape = (
        longer,
        longer,
        jax.ShapeDtypeStruct((len(offsets) * block, dim), BF16),
        jax.ShapeDtypeStruct((len(offsets), 1, block), F32),
    )
    return pl.pallas_call(
        functools.partial(denom_kernel, n, offsets),
        grid=(comps // tile,),
        out_shape=out_shape,
        in_specs=[
            pl.BlockSpec((tile, dim), lambda i: (i, 0)),
            pl.BlockSpec((1, 1, tile), lambda i: (i, 0, 0)),
            pl.BlockSpec(memory_space=pl.ANY),
            whole((n, 1, block)),
            whole((half, dim)),
            whole((half, dim)),
        ],
        out_specs=tuple(whole(o.shape) for o in out_shape),
        scratch_shapes=[
            pltpu.VMEM((1, 2 * half), F32),
            pltpu.SemaphoreType.DMA((len(offsets),)),
        ],
        compiler_params=params(40),
        cost_estimate=cost(2 * half * comps * dim, 2 * (comps + 2 * half) * dim, 2 * half * comps),
        name="denominators",
    )(cen, lw.reshape(comps // tile, 1, tile), cen, lw.reshape(n, 1, block), ua, ub)


def sums_kernel(first, last, half, at, c_ref, lw_ref, tail_ref, *refs):
    pieces, refs = refs[:2], refs[2:]
    if not first:
        acc_in, cnt_in, refs = refs[0], refs[1], refs[2:]
    *outs, cnt_out = refs
    block = c_ref.shape[0] // lw_ref.shape[0]
    comps = slice(at, at + sum(out.shape[0] for out in outs))
    shift = jnp.concatenate(
        [column(lw_ref[q]) for q in range(comps.start // block, comps.stop // block)], 0
    )
    c = c_ref[comps, :]
    rows = 2 * half
    end = tail_ref.shape[0]
    tail = tail_ref[end - TAIL : end, : 2 * rows].astype(F32)[:1]
    weight = tail[:, :rows] + tail[:, rows:]
    count, total = None, None
    for i, piece in enumerate(pieces):
        u = piece[:half, :]
        resp = []
        for j, e in enumerate(exp_scores(c, u, shift)):
            lanes = i * half + j * LANES
            r = (e * weight[:, lanes : lanes + LANES]).astype(BF16)
            count = r.astype(F32) if count is None else count + r.astype(F32)
            resp.append(r)
        part = jnp.dot(jnp.concatenate(resp, 1), u, preferred_element_type=F32)
        total = part if total is None else total + part
    if not first:
        total = total + acc_in[comps, :]
        count = count + cnt_in[comps, :]
    start = 0
    for out in outs:
        out[...] = total[start : start + out.shape[0], :]
        start += out.shape[0]
    if last:
        for q in range(cnt_out.shape[0]):
            one = count[q * block : (q + 1) * block, :]
            cnt_out[q : q + 1, :] = jnp.sum(one.T, 0, keepdims=True)
    else:
        cnt_out[...] = count


def sums(cen, lw, tail, pieces, half, state, segment=None):
    comps, dim = cen.shape
    last = segment is not None
    first = state is None
    if last:
        at, size = segment
        block = lw.shape[2]
        out_shape = (jax.ShapeDtypeStruct((size // 2, dim), F32),) * 2
        out_shape += (jax.ShapeDtypeStruct((size // block, block), F32),)
    else:
        at, size = 0, comps
        out_shape = (
            jax.ShapeDtypeStruct((comps, dim), F32),
            jax.ShapeDtypeStruct((comps, LANES), F32),
        )
    args = [cen, lw, tail, *pieces] + ([] if first else list(state))
    aliases = {} if first or last else {len(args) - 2: 0, len(args) - 1: 1}
    return pl.pallas_call(
        functools.partial(sums_kernel, first, last, half, at),
        out_shape=out_shape,
        in_specs=[VMEM] * len(args),
        out_specs=(VMEM,) * len(out_shape),
        input_output_aliases=aliases,
        compiler_params=params(24),
        cost_estimate=cost(4 * half * size * dim, 2 * (size + 2 * half) * dim, 2 * half * size),
        name="sums",
    )(*args)


def merge_kernel(terms, n_in, *refs):
    arrays, outs = refs[:n_in], refs[n_in:]
    for out, parts in zip(outs, terms):
        total = sum(arrays[i][at : at + out.shape[0], :].astype(F32) for i, at in parts)
        out[...] = total.astype(out.dtype)


def normalize(x):
    return x * lax.rsqrt(jnp.sum(x * x, 1, keepdims=True) + EPS)


def directions_kernel(terms, size, *refs):
    *arrays, out = refs
    for k, parts in enumerate(terms):
        total = sum(arrays[i][at : at + size, :].astype(F32) for i, at in parts)
        out[k * size : (k + 1) * size, :] = normalize(total).astype(out.dtype)


def directions(wanted, size):
    arrays, terms = distinct(wanted)
    dim = arrays[0].shape[1]
    return pl.pallas_call(
        functools.partial(directions_kernel, terms, size),
        out_shape=jax.ShapeDtypeStruct((size * len(wanted), dim), BF16),
        in_specs=[VMEM] * len(arrays),
        out_specs=VMEM,
        compiler_params=params(8),
        cost_estimate=cost(0, 12 * size * dim * len(wanted), size),
        name="directions",
    )(*arrays)


def distinct(wanted):
    arrays, terms = [], []
    for parts in wanted:
        term = []
        for x, at in parts:
            if not any(x is y for y in arrays):
                arrays.append(x)
            term.append((next(i for i, y in enumerate(arrays) if y is x), at))
        terms.append(term)
    return arrays, terms


def merge(wanted, sizes):
    arrays, terms = distinct(wanted)
    dim = arrays[0].shape[1]
    return pl.pallas_call(
        functools.partial(merge_kernel, terms, len(arrays)),
        out_shape=tuple(jax.ShapeDtypeStruct((size, dim), BF16) for size in sizes),
        in_specs=[VMEM] * len(arrays),
        out_specs=(VMEM,) * len(wanted),
        compiler_params=params(8),
        cost_estimate=cost(0, 12 * sum(sizes) * dim, sum(sizes)),
        name="merge",
    )(*arrays)


def normalizer_kernel(n_comps, lw_rows, n_rows, half, *refs):
    comps, refs = refs[:n_comps], refs[n_comps:]
    lw_ref, refs = refs[0], refs[1:]
    pieces, refs = refs[: 2 * n_rows], refs[2 * n_rows :]
    before, outs = refs[:-n_rows], refs[-n_rows:]
    c = jnp.concatenate([r[...] for r in comps], 0)
    shift = jnp.concatenate(
        [
            column(lw_ref[q : q + 1, :])[h * r.shape[0] : (h + 1) * r.shape[0], :]
            for r, (q, h) in zip(comps, lw_rows)
        ],
        0,
    )
    for i, out in enumerate(outs):
        for k in range(2):
            s = jnp.concatenate(
                [
                    jnp.sum(p, 0, keepdims=True)
                    for p in exp_scores(c, pieces[2 * i + k][:half, :], shift)
                ],
                1,
            )
            at = slice(None), slice(k * half, (k + 1) * half)
            out[at] = before[i][at] + s if before else s


def normalizers(comps, lw, lw_rows, before, pieces, half):
    dim = pieces[0].shape[1]
    n_comps, n_rows = sum(c.shape[0] for c in comps), len(pieces) // 2
    args = [*comps, lw, *pieces, *before]
    rows = 2 * half * n_rows
    return pl.pallas_call(
        functools.partial(normalizer_kernel, len(comps), lw_rows, n_rows, half),
        out_shape=(jax.ShapeDtypeStruct((1, 2 * half), F32),) * n_rows,
        in_specs=[VMEM] * len(args),
        out_specs=(VMEM,) * n_rows,
        compiler_params=params(12),
        cost_estimate=cost(rows * n_comps * dim, 2 * (n_comps + rows) * dim, rows * n_comps),
        name="normalizers",
    )(*args)


def local(embeddings, centroids, log_weights):
    n = lax.axis_size("rows")
    comps, dim = centroids.shape
    block = comps // n
    half = embeddings.shape[0] // 2
    row_total = embeddings.shape[0] * n
    me = lax.axis_index("rows")
    across, along = 1 << ACROSS, 1 << ALONG
    far = [1 << b for b in range(n.bit_length() - 1) if b not in (ACROSS, ALONG)]

    def after(terms, ready):
        *others, (x, at) = terms
        x, _ = lax.optimization_barrier((x, ready))
        return [*others, (x, at)]

    def swap(x, mask):
        return lax.ppermute(x, "rows", [(i, i ^ mask) for i in range(n)])

    offsets = [0]
    for mask in far:
        offsets = [o | m for o in offsets for m in (0, mask)]
    where = {o: q for q, o in enumerate(offsets)}

    ua, ub = unit(embeddings)
    xb, za = swap(ub, across), swap(ua, along)
    va, vb, cen, lw = denominators(centroids, log_weights, ua, ub, n, offsets)
    xa, zb = swap(va, across), swap(vb, along)
    da, db = swap(za, across), swap(xb, along)
    d_tail = swap(zb[half:], across)

    state = sums(cen, lw, va, (va, vb), half, None)
    state = sums(cen, lw, xa, (xa, xb), half, state)
    state = sums(cen, lw, zb, (za, zb), half, state)
    size = len(offsets) // 2 * block
    send0, send1, send_counts = sums(cen, lw, d_tail, (da, db), half, state, (size, size))
    keep0, keep1, keep_counts = sums(cen, lw, d_tail, (da, db), half, state, (0, size))

    got1 = swap(send1, far[0])
    got0 = swap(send0, far[0])
    quarter = len(offsets) // 4
    sub = block // PARTS
    parts = {}
    for pair, first in (((keep0, got0), 0), ((keep1, got1), quarter)):
        for q in range(quarter):
            for h in range(PARTS):
                parts[offsets[first + q], h] = [(x, q * block + h * sub) for x in pair]
    ready, done = None, []
    for k, mask in list(enumerate(far))[1:]:
        leaving = [o for o in reversed(offsets) if (o, 0) in parts and o & mask]
        items = [(o, h) for o in leaving for h in range(PARTS)]
        if k == 1 < len(far) - 1:
            items = [(o, h) for o, h in items if o != mask or h == 0]
        for group in [items] if k == 1 else [[i] for i in items]:
            sizes = [block if o == mask and k == 1 < len(far) - 1 else sub for o, h in group]
            wanted = [parts[i] for i in group]
            if ready is not None:
                wanted[0] = after(wanted[0], ready)
            merged = merge(wanted, sizes)
            done.append(merged[0])
            if k > 1:
                ready = merged[0]
            for (o, h), x, size in zip(group, merged, sizes):
                x = swap(x, mask)
                for i in range(size // sub):
                    parts.pop((o, h + i))
                    parts[o ^ mask, h + i].append((x, i * sub))
    dirs = {}
    for h in range(PARTS):
        wanted = parts[0, h] if h == 0 else after(parts[0, h], dirs[0, h - 1])
        dirs[0, h] = directions([wanted], sub)
    own_dirs = jnp.concatenate([dirs[0, h] for h in range(PARTS)])

    counts = jnp.concatenate([keep_counts, send_counts])
    points = [done[0], done[min(1, len(done) - 1)], dirs[0, 0]]
    for k, mask in enumerate(far):
        counts, _ = lax.optimization_barrier((counts, points[min(k, 2)]))
        order = [where[o ^ mask] for o in offsets]
        got = swap(counts, mask)
        counts = counts + jnp.concatenate([got[q : q + 1] for q in order])
    new_lw = jnp.log(counts / row_total)
    own_lw = new_lw[0]

    halves = range(PARTS)
    for mask in reversed(far[2:]):
        for o, h in list(dirs):
            dirs[o | mask, h] = swap(dirs[o, h], mask)
    pieces = (va, vb, xa, xb, za, zb, da, db)
    total = ()

    def send(o, h, mask, ready=None):
        x = dirs[o, h]
        if ready is not None:
            x, _ = lax.optimization_barrier((x, ready))
            dirs[o, h] = x
        dirs[o | mask, h] = swap(x, mask)

    def use(o, hs, total, rows=None):
        keys = [(p, h) for p in (o, o | far[0]) for h in hs]
        places = [(where[p], h) for p, h in keys]
        return normalizers([dirs[k] for k in keys], new_lw, places, total, rows or pieces, half)

    near, *outer = [o for o in offsets if not o & (far[0] | far[1])]
    for h in halves:
        send(near, h, far[1])
        send(near, h, far[0])
    total = use(near, halves, total)
    for o in outer:
        for h in halves:
            send(o, h, far[1], total[0] if h == 0 else dirs[o | far[0], h - 1])
            send(o, h, far[0])
    for h in halves:
        send(near | far[1], h, far[0], dirs[outer[0], 0] if outer else None)
    total = use(near | far[1], halves, total)
    for o in outer:
        first, total = lax.optimization_barrier((dirs[o | far[1], 0], total))
        dirs[o | far[1], 0] = first
        send(o | far[1], 0, far[0])
        total = use(o, halves, total)
    for o in outer:
        for h in halves[1:]:
            send(o | far[1], h, far[0], total[0])
        (own,), others = total[:1], total[1:]
        others = use(o | far[1], halves, others, pieces[2:])
        total = (*use(o | far[1], halves, (own,), pieces[:2]), *others)

    own, x, z, d = total
    whole = own + swap(d, across | along) + swap(z, along) + swap(x, across)
    return own_dirs, own_lw, jnp.log(whole[0])


def solution(mesh):
    return jax.shard_map(
        local,
        mesh=mesh,
        in_specs=(P(("grp", "rows"), None), P(), P()),
        out_specs=(P(("grp", "rows"), None), P(("grp", "rows")), P(("grp", "rows"))),
        check_vma=False,
    )
```
